32 devices in a mesh: shot: 8 (over y, x, core), rbin: 4 (over z).
Axes of the slice: x: 2, y: 2, z: 4, core: 2. Of those that a mesh axis runs over, the one named last changes fastest.
Arguments:
- local_gathers: bfloat16 [2, 2, 4096, 1024], P(None, None, 'shot', 'rbin'), may hold values from -6 to 6
- recorded_shots: bfloat16 [8, 2, 2, 256, 2048], P('shot', None, None, 'rbin'), may hold values from -0.25 to 0.25
- block_owner: int32 [4], replicated, may hold values from 0 to 7, as said below
- aperture_start: int32 [4096], P('shot'), may hold values from 0 to 1023, as said below
- aperture_end: int32 [4096], P('shot'), may hold values from 1 to 1024
- taper_bin: int32 [1024], P('rbin'), may hold values from 0 to 7
- taper_gain: float32 [8], replicated, may hold values from 0.25 to 1
Outputs:
- multiples: float32 [2, 2048, 2, 4096], P(None, 'rbin', None, 'shot')
The draws below stay inside these ranges and needn't reach their ends.
Inputs may be any that keep to these rules, and one draw needn't show every extreme that they name: `block_owner`: the 4 entries are distinct. aperture_start < aperture_end for every shot.
All inputs are finite; a program needn't handle non-finite values.
Results may differ from the reference program's by a relative error of at most 0.0029.
Values may be sent and summed in bfloat16 or wider, within the bound.
No kernel may reach another device: no remote copies, remote signals or barrier semaphores. Data moves between devices by JAX's collectives and lax.ppermute only.
A program may use at most 128 MiB of HBM per device.

```python
import jax
import jax.numpy as jnp
from jax import lax

RECEIVERS = 2048
FREQS = 2
BLOCKS = 4
TAPER_BINS = 8
SHOTS = 4096
POINTS = 1024
BLOCK_POINTS = 64
EDGE = 64
SLOTS = 8
N_RBIN = 4


def aperture_pair(key):
    centre_point = jax.random.randint(jax.random.fold_in(key, 11), (SHOTS,), 0, POINTS)
    half_width = jax.random.randint(jax.random.fold_in(key, 12), (SHOTS,), POINTS // 16, POINTS // 4 + 1)
    starting = jnp.maximum(centre_point - half_width, 0)
    ending = jnp.minimum(centre_point + half_width, POINTS)
    starting = starting.at[0].set(0)
    ending = ending.at[SHOTS - 1].set(POINTS)
    starting = starting.at[1].set(0)
    ending = ending.at[1].set(1)
    starting = starting.at[SHOTS - 2].set(POINTS - 1)
    ending = ending.at[SHOTS - 2].set(POINTS)
    return (starting.astype(jnp.int32), ending.astype(jnp.int32))


def draw_aperture_start(key, part):
    return aperture_pair(key)[0]


def draw_aperture_end(key, part):
    return aperture_pair(key)[1]


def draw_block_owner(key, part):
    middle = 1 + jax.random.permutation(jax.random.fold_in(key, 21), SLOTS - 2)[:BLOCKS - 2]
    endings = jnp.array([0, SLOTS - 1], jnp.int32)
    together = jnp.concatenate([endings, middle.astype(jnp.int32)])
    return jax.random.permutation(jax.random.fold_in(key, 22), together).astype(jnp.int32)


def touch_ends(entries, stream_key, least, largest):
    longest = entries.shape.index(max(entries.shape))
    spots = []
    for shift in (0, 1):
        where = [jax.random.randint(jax.random.fold_in(stream_key, axis), (), 0, length) for axis, length in enumerate(entries.shape)]
        where[longest] = (where[longest] + shift) % entries.shape[longest]
        spots.append(tuple(where))
    return entries.at[spots[0]].set(least).at[spots[1]].set(largest)


def spiked(values, key, source, target, parts, factor):
    def block_of(position):
        return (jnp.arange(values.shape[position]) // (values.shape[position] // parts)).reshape((-1,) + (1,) * (values.ndim - 1 - position))

    one_side = jax.random.permutation(key, parts)[block_of(target)]
    second = (block_of(target) + parts // 2) % parts
    return jnp.where((block_of(source) == one_side) | (block_of(source) == second), factor * values, values)


def shard_levels(key, extent, split, least, largest):
    def one(dim, parts):
        draws = jax.random.uniform(jax.random.fold_in(jax.random.fold_in(key, 6), dim), (parts,), jnp.float32, least / len(split), largest / len(split))
        return jnp.repeat(jnp.exp(draws), extent[dim] // parts).reshape((-1,) + (1,) * (len(extent) - dim - 1))

    factor_of = one(*split[0])
    for cut in split[1:]:
        factor_of = factor_of * one(*cut)
    return factor_of


def normal_values(stream_key, extent, scale, most, cuts=(), kind=jnp.bfloat16):
    loudness = shard_levels(stream_key, extent, cuts, -0.22, 0.18) if cuts else 1.0
    values = jax.random.normal(stream_key, extent, jnp.float32) * scale * loudness
    return jnp.minimum(jnp.maximum(values, -most), most).astype(kind)


def bell_draw_with(key, dims, width, most, cuts, heavy, kind=jnp.bfloat16):
    values = width * jax.random.normal(key, dims, jnp.float32)
    if cuts:
        values = values * shard_levels(key, dims, cuts, -0.22, 0.18)
    return jnp.clip(spiked(values, jax.random.fold_in(key, 3), *heavy), -most, most).astype(kind)


def setup_inputs(seed: int = 0) -> dict:
    splits = jax.random.split(jax.random.key(seed), 8)
    local_gathers = normal_values(splits[0], (FREQS, 2, SHOTS, POINTS), 1.0, 6.0, ((2, 8), (3, 4)))
    recorded_shots = bell_draw_with(splits[1], (SLOTS, FREQS, 2, BLOCK_POINTS * N_RBIN, RECEIVERS), POINTS ** -0.5, 0.25, ((0, 8), (3, 4)), (3, 4, 4, 2.0))
    block_owner = draw_block_owner(jax.random.fold_in(splits[7], 71), 0)
    aperture_start = draw_aperture_start(jax.random.fold_in(splits[7], 71), 0)
    aperture_end = draw_aperture_end(jax.random.fold_in(splits[7], 71), 0)
    taper_bin = touch_ends(jax.random.randint(splits[5], (POINTS,), 0, TAPER_BINS), jax.random.fold_in(splits[5], 1), 0, TAPER_BINS - 1).astype(jnp.int32)
    taper_gain = jnp.clip(jax.random.uniform(splits[6], (TAPER_BINS,), jnp.float32, 0.25, 1.0), 0.25, 1.0)
    return {"local_gathers": local_gathers, "recorded_shots": recorded_shots, "block_owner": block_owner, "aperture_start": aperture_start, "aperture_end": aperture_end, "taper_bin": taper_bin, "taper_gain": taper_gain}


def taper_weights(aperture_start, aperture_end, taper_bin, taper_gain):
    columns = jnp.arange(POINTS, dtype=jnp.int32)
    inside = (columns[None, :] >= aperture_start[:, None]) & (columns[None, :] < aperture_end[:, None])
    distance = jnp.minimum(columns[None, :] - aperture_start[:, None], aperture_end[:, None] - 1 - columns[None, :])
    ramped = jnp.minimum((distance + 1).astype(jnp.float32) / EDGE, 1.0)
    return jnp.where(inside, ramped, 0.0) * taper_gain[taper_bin][None, :]


def reference(local_gathers, recorded_shots, block_owner, aperture_start, aperture_end, taper_bin, taper_gain):
    weight = taper_weights(aperture_start, aperture_end, taper_bin, taper_gain)
    tapered = (local_gathers.astype(jnp.float32) * weight[None, None]).astype(jnp.bfloat16)
    grouped = tapered.reshape(FREQS, 2, SHOTS, N_RBIN, BLOCKS, BLOCK_POINTS)
    accumulated = jnp.zeros((FREQS, RECEIVERS, 2, SHOTS), jnp.float32)
    for block_index in range(BLOCKS):
        received = lax.dynamic_index_in_dim(recorded_shots, block_owner[block_index], 0, keepdims=False).astype(jnp.float32)
        picked = grouped[:, :, :, :, block_index, :].reshape(FREQS, 2, SHOTS, N_RBIN * BLOCK_POINTS).astype(jnp.float32)
        real_part = jnp.einsum("fsx,fxr->frs", picked[:, 0], received[:, 0]) - jnp.einsum("fsx,fxr->frs", picked[:, 1], received[:, 1])
        imag_part = jnp.einsum("fsx,fxr->frs", picked[:, 0], received[:, 1]) + jnp.einsum("fsx,fxr->frs", picked[:, 1], received[:, 0])
        accumulated = accumulated + jnp.stack([real_part, imag_part], axis=2)
    return -accumulated
```

```python
import jax
import jax.numpy as jnp
from jax import lax
from jax.sharding import PartitionSpec as P

BLOCKS = 4
EDGE = 64


def taper_weights(columns, aperture_start, aperture_end, taper_bin, taper_gain):
    inside = (columns[None, :] >= aperture_start[:, None]) & (
        columns[None, :] < aperture_end[:, None]
    )
    distance = jnp.minimum(
        columns[None, :] - aperture_start[:, None], aperture_end[:, None] - 1 - columns[None, :]
    )
    ramped = jnp.minimum((distance + 1).astype(jnp.float32) / EDGE, 1.0)
    labels = jnp.arange(taper_gain.shape[0], dtype=jnp.int32)
    bin_gain = jnp.sum(
        jnp.where(taper_bin[:, None] == labels[None, :], taper_gain[None, :], 0.0), axis=1
    )
    return jnp.where(inside, ramped, 0.0) * bin_gain[None, :]


def per_device(
    local_gathers, recorded_shots, block_owner, aperture_start, aperture_end, taper_bin, taper_gain
):
    freqs, _, shots, points = local_gathers.shape
    rows, receivers = recorded_shots.shape[3:]
    slots = lax.axis_size("shot")
    bins = lax.axis_size("rbin")
    own = receivers // bins
    parts = slots // (2 * freqs)
    part = own // parts

    columns = lax.axis_index("rbin") * points + jnp.arange(points, dtype=jnp.int32)
    weight = taper_weights(columns, aperture_start, aperture_end, taper_bin, taper_gain)
    tapered = (local_gathers.astype(jnp.float32) * -weight[None, None]).astype(jnp.bfloat16)
    gathers = lax.all_gather(tapered, "rbin")

    shares = recorded_shots[0].reshape(freqs, 2, rows, bins, parts, part)
    shares = shares.transpose(0, 1, 4, 3, 2, 5).reshape(slots, bins, rows, part)
    shares = lax.all_to_all(shares, "shot", 0, 0)
    picked = jnp.take(shares, block_owner, axis=0).transpose(1, 0, 2, 3)
    picked = lax.all_to_all(picked, "rbin", 0, 0)
    picked = picked.reshape(bins * BLOCKS * rows, part).T
    recorded = lax.all_gather(picked, "shot").reshape(freqs, 2, own, bins * points)

    real = recorded[:, 0]
    imag = recorded[:, 1]
    g = gathers.transpose(1, 2, 3, 0, 4).reshape(freqs, 2, shots, bins * points)

    def dot(a, b):
        return lax.dot_general(a, b, (((2,), (2,)), ((0,), (0,))), preferred_element_type=jnp.float32)

    out_real = dot(real, g[:, 0]) - dot(imag, g[:, 1])
    out_imag = dot(real, g[:, 1]) + dot(imag, g[:, 0])
    return jnp.stack([out_real, out_imag], axis=2)


def solution(mesh):
    in_specs = (
        P(None, None, "shot", "rbin"),
        P("shot", None, None, "rbin", None),
        P(),
        P("shot"),
        P("shot"),
        P("rbin"),
        P(),
    )
    out_specs = P(None, "rbin", None, "shot")
    return jax.shard_map(
        per_device, mesh=mesh, in_specs=in_specs, out_specs=out_specs, check_vma=False
    )
```

```python
import functools

import jax
import jax.numpy as jnp
from jax import lax
from jax.experimental import pallas as pl
from jax.experimental.pallas import tpu as pltpu
from jax.sharding import PartitionSpec as P

BLOCKS = 4
EDGE = 64
ROWS = 256
EARLY_BYTES = 40 * 2**20
LATE_BYTES = 16 * 2**20
ROWS_BY_ROWS = (((1,), (1,)), ((), ()))
WHOLE = pl.BlockSpec(memory_space=pltpu.VMEM)
SCALARS = pl.BlockSpec(memory_space=pltpu.SMEM)
IN_PLACE = pl.BlockSpec(memory_space=pl.ANY)


def exchange(value, axis, distance, among=None):
    pairs = [(i ^ distance, i) for i in range(lax.axis_size(axis))]
    return lax.ppermute(value, axis, [p for p in pairs if among is None or p in among])


def after(value, *earlier):
    return lax.optimization_barrier((value, earlier))[0]


def taper_kernel(first_ref, gain_ref, start_ref, end_ref, bin_ref, origin_ref, gathers_ref, tapered_ref):
    shots, points = gathers_ref.shape[2:]
    origins = origin_ref[...] == lax.broadcasted_iota(jnp.int32, (points, points), 0)
    origins = origins.astype(jnp.float32).astype(jnp.bfloat16)
    labels = bin_ref[...]
    column = first_ref[0] + lax.broadcasted_iota(jnp.int32, labels.shape, 1)
    gain = jnp.zeros(labels.shape, jnp.float32)
    for label in range(gain_ref.shape[0]):
        gain = gain + jnp.where(labels == label, gain_ref[label], 0.0)
    start = jnp.broadcast_to(start_ref[...], (128, shots)).T[:, :1]
    end = jnp.broadcast_to(end_ref[...], (128, shots)).T[:, :1]
    distance = jnp.minimum(column - start, end - 1 - column)
    ramped = jnp.minimum((distance + 1).astype(jnp.float32) / EDGE, 1.0)
    weight = jnp.where(distance >= 0, ramped, 0.0) * -gain
    for freq in range(gathers_ref.shape[0]):
        for part in range(2):
            value = (gathers_ref[freq, part].astype(jnp.float32) * weight).astype(jnp.bfloat16)
            value = jnp.dot(value, origins, preferred_element_type=jnp.float32).astype(jnp.bfloat16)
            tapered_ref[freq, part] = value


def taper(gathers, aperture_start, aperture_end, taper_bin, taper_gain, origin):
    shots, points = gathers.shape[2:]
    first = (lax.axis_index("rbin") * points).reshape(1)
    return pl.pallas_call(
        taper_kernel,
        in_specs=[SCALARS, SCALARS, WHOLE, WHOLE, WHOLE, WHOLE, WHOLE],
        out_specs=WHOLE,
        out_shape=jax.ShapeDtypeStruct(gathers.shape, jnp.bfloat16),
        name="taper",
    )(
        first,
        taper_gain,
        aperture_start.reshape(1, shots),
        aperture_end.reshape(1, shots),
        taper_bin.reshape(1, points),
        origin.reshape(1, points),
        gathers,
    )


def transpose_kernel(me_ref, picked_ref, out_ref):
    bins, blocks, rows, own = picked_ref.shape
    width = blocks * rows
    for unit in range(bins):
        values = picked_ref[lax.bitwise_xor(me_ref[1], unit)].reshape(width, own)
        out_ref[:, unit * width : (unit + 1) * width] = values.T


def unit_product(r0, r1, g):
    def dot(a, b):
        return lax.dot_general(a, b, ROWS_BY_ROWS, preferred_element_type=jnp.float32)

    return dot(r0, g[0]) + dot(-r1, g[1]), dot(r0, g[1]) + dot(r1, g[0])


def choose(rbin, bins, freq, refs):
    values = [ref[freq] if len(ref.shape) == 4 else ref[...] for ref in refs]
    if len(values) == 1:
        return values[0]
    inner = jnp.logical_and(rbin > 0, rbin < bins - 1)
    return jnp.where(inner, values[0], values[1])


def early_kernel(order, n_operands, n_pieces, me_ref, *refs):
    refs = list(refs)
    piece_refs = [refs.pop(0) for _ in range(n_pieces)]
    operands = [refs.pop(0) for _ in range(n_operands)]
    units = [[[operands[i] for i in unit] for unit in of_freq] for of_freq in order]
    out_ref, real_ref, imag_ref, left_ref, held, done, in_sems, out_sems = refs
    shot, rbin = me_ref[0], me_ref[1]
    copies = [
        pltpu.make_async_copy(ref, held.at[lax.bitwise_xor(shot, d)], in_sems.at[d])
        for d, ref in enumerate(piece_refs)
    ]
    for copy in copies:
        copy.start()
    for copy in copies:
        copy.wait()
    freqs = out_ref.shape[0]
    bins = max(len(of_freq) for of_freq in order)
    parts = n_pieces // (2 * freqs)
    own, width = held.shape[1], held.shape[2] // bins

    def recorded(freq, part, here, unit):
        span = slice(unit * width, (unit + 1) * width)
        first = (freq * 2 + part) * parts
        return jnp.concatenate([held[first + h, here, span] for h in range(parts)], axis=1)

    rows = min(own, ROWS)
    leaving = []
    for freq, of_freq in enumerate(units):
        for chunk in range(own // rows):
            here = slice(chunk * rows, (chunk + 1) * rows)
            real = imag = None
            for unit, candidates in enumerate(of_freq):
                g = choose(rbin, bins, freq, candidates)
                r0, r1 = recorded(freq, 0, here, unit), recorded(freq, 1, here, unit)
                a, b = unit_product(r0, r1, g)
                real = a if real is None else real + a
                imag = b if imag is None else imag + b
            if freq < freqs - 1:
                done[freq, here, 0, :] = real
                done[freq, here, 1, :] = imag
                leaving.append(
                    pltpu.make_async_copy(
                        done.at[freq, here], out_ref.at[freq, here], out_sems.at[freq, chunk]
                    )
                )
                leaving[-1].start()
            else:
                real_ref[here] = real
                imag_ref[here] = imag
                for part in range(2):
                    left_ref[part, here] = recorded(freq, part, here, bins - 1)
    for copy in leaving:
        copy.wait()


def late_kernel(bins, n_candidates, me_ref, *refs):
    candidates = refs[:n_candidates]
    real_ref, imag_ref, left_ref, _, out_ref, done, sems = refs[n_candidates:]
    freq = out_ref.shape[0] - 1
    g = choose(me_ref[1], bins, freq, candidates)
    chunks = sems.shape[0]
    rows = real_ref.shape[0] // chunks
    leaving = []
    for chunk in range(chunks):
        here = slice(chunk * rows, (chunk + 1) * rows)
        a, b = unit_product(left_ref[0, here], left_ref[1, here], g)
        done[here, 0, :] = real_ref[here] + a
        done[here, 1, :] = imag_ref[here] + b
        leaving.append(
            pltpu.make_async_copy(done.at[here], out_ref.at[freq, here], sems.at[chunk])
        )
        leaving[-1].start()
    for copy in leaving:
        copy.wait()


def product(me, pieces, gathers):
    freqs, bins = len(gathers), len(gathers[0])
    shots, points = gathers[0][0][0].shape[-2:]
    n_pieces, (own, held_points) = len(pieces), pieces[0].shape
    chunks = own // min(own, ROWS)
    *full, last = gathers
    operands, order = [], []
    for of_freq in [*full, last[:-1]]:
        order.append([])
        for unit in of_freq:
            for value in unit:
                if not any(value is known for known in operands):
                    operands.append(value)
            order[-1].append([[value is o for o in operands].index(True) for value in unit])
    out_type = jax.ShapeDtypeStruct((freqs, own, 2, shots), jnp.float32)
    sum_type = jax.ShapeDtypeStruct((own, shots), jnp.float32)
    out, real, imag, left = pl.pallas_call(
        functools.partial(early_kernel, order, len(operands), n_pieces),
        in_specs=[SCALARS] + [IN_PLACE] * n_pieces + [WHOLE] * len(operands),
        out_specs=[IN_PLACE, WHOLE, WHOLE, WHOLE],
        out_shape=[
            out_type,
            sum_type,
            sum_type,
            jax.ShapeDtypeStruct((2, own, points), jnp.bfloat16),
        ],
        scratch_shapes=[
            pltpu.VMEM((n_pieces, own, held_points), jnp.bfloat16),
            pltpu.VMEM((freqs - 1, own, 2, shots), jnp.float32),
            pltpu.SemaphoreType.DMA((n_pieces,)),
            pltpu.SemaphoreType.DMA((freqs - 1, chunks)),
        ],
        compiler_params=pltpu.CompilerParams(vmem_limit_bytes=EARLY_BYTES),
        name="early",
    )(me, *pieces, *operands)
    n_last = len(last[-1])
    return pl.pallas_call(
        functools.partial(late_kernel, bins, n_last),
        in_specs=[SCALARS] + [WHOLE] * (n_last + 3) + [IN_PLACE],
        out_specs=IN_PLACE,
        out_shape=out_type,
        scratch_shapes=[
            pltpu.VMEM((own, 2, shots), jnp.float32),
            pltpu.SemaphoreType.DMA((chunks,)),
        ],
        input_output_aliases={n_last + 4: 0},
        compiler_params=pltpu.CompilerParams(vmem_limit_bytes=LATE_BYTES),
        name="late",
    )(me, *last[-1], real, imag, left, out)


def per_device(
    local_gathers, recorded_shots, block_owner, aperture_start, aperture_end, taper_bin, taper_gain
):
    freqs, _, shots, points = local_gathers.shape
    rows, receivers = recorded_shots.shape[3:]
    slots = lax.axis_size("shot")
    bins = lax.axis_size("rbin")
    rbin = lax.axis_index("rbin")
    own = receivers // bins
    parts = slots // (2 * freqs)
    width = rows // parts

    shares = lax.all_to_all(recorded_shots[0].reshape(slots, width, receivers), "shot", 0, 0)
    picked = shares[block_owner].reshape(BLOCKS, width, bins, own).transpose(2, 0, 1, 3)

    origin = jnp.arange(points, dtype=jnp.int32).reshape(BLOCKS, parts, width).transpose(1, 0, 2)
    me = jnp.stack([lax.axis_index("shot"), lax.axis_index("rbin")]).astype(jnp.int32)
    tapered = taper(
        local_gathers, aperture_start, aperture_end, taper_bin, taper_gain, origin
    )
    if bins == 4:
        inner, outward = [(1, 2), (2, 1)], [(1, 0), (2, 3)]
        near = exchange(tapered, "rbin", 1)
        across = exchange(tapered, "rbin", 3, inner)
        picked = lax.all_to_all(after(picked, near, across), "rbin", 0, 0)
        second = exchange(across, "rbin", 1, outward)
        gathers = []
        ready, sent = picked, ()
        for freq in range(freqs):
            crossed = exchange(after(near, ready)[freq], "rbin", 3, inner)
            passed = exchange(after(crossed, sent), "rbin", 1, outward)
            gathers.append([[tapered], [near], [crossed, second], [across, passed]])
            ready, sent = crossed, passed
    else:
        picked = lax.all_to_all(picked, "rbin", 0, 0)
        gathers = [[[tapered]] + [[exchange(tapered, "rbin", d)] for d in range(1, bins)]] * freqs

    piece = pl.pallas_call(
        transpose_kernel,
        in_specs=[SCALARS, WHOLE],
        out_specs=WHOLE,
        out_shape=jax.ShapeDtypeStruct((own, bins * BLOCKS * width), jnp.bfloat16),
        name="turn",
    )(me, picked)
    pieces = []
    for d in range(0, slots, 2):
        other = piece if d == 0 else exchange(piece, "shot", d)
        pieces += [other, exchange(other, "shot", 1)]
    return product(me, pieces, gathers)


def solution(mesh):
    in_specs = (
        P(None, None, "shot", "rbin"),
        P("shot", None, None, "rbin", None),
        P(),
        P("shot"),
        P("shot"),
        P("rbin"),
        P(),
    )
    out_specs = P(None, "rbin", None, "shot")
    return jax.shard_map(
        per_device, mesh=mesh, in_specs=in_specs, out_specs=out_specs, check_vma=False
    )
```

```python
import functools

import jax
import jax.numpy as jnp
import numpy as np
from jax import lax
from jax.experimental import pallas as pl
from jax.experimental.pallas import tpu as pltpu
from jax.sharding import PartitionSpec as P

BLOCKS = 4
EDGE = 64
ROWS = 256
PICK_FLOPS = 2 * 10**10
EARLY_FLOPS = 4 * 10**9
EARLY_BYTES = 40 * 2**20
LATE_BYTES = 16 * 2**20
ROWS_BY_ROWS = (((1,), (1,)), ((), ()))
WHOLE = pl.BlockSpec(memory_space=pltpu.VMEM)
SCALARS = pl.BlockSpec(memory_space=pltpu.SMEM)
IN_PLACE = pl.BlockSpec(memory_space=pl.ANY)


def exchange(value, axis, distance, among=None):
    pairs = [(i ^ distance, i) for i in range(lax.axis_size(axis))]
    return lax.ppermute(value, axis, [p for p in pairs if among is None or p in among])


def cost(flops):
    return pl.CostEstimate(flops=flops, bytes_accessed=2**21, transcendentals=0)


def after(value, *earlier):
    return lax.optimization_barrier((value, earlier))[0]


def taper_kernel(gain_ref, start_ref, end_ref, bin_ref, origin_ref, gathers_ref, tapered_ref):
    shots, points = gathers_ref.shape[2:]
    origins = origin_ref[...] == lax.broadcasted_iota(jnp.int32, (points, points), 0)
    origins = origins.astype(jnp.float32).astype(jnp.bfloat16)
    labels = bin_ref[...]
    first = lax.axis_index("rbin") * points
    column = first + lax.broadcasted_iota(jnp.int32, labels.shape, 1)
    gain = jnp.zeros(labels.shape, jnp.float32)
    for label in range(gain_ref.shape[0]):
        gain = gain + jnp.where(labels == label, gain_ref[label], 0.0)
    start = jnp.broadcast_to(start_ref[...], (128, shots)).T[:, :1]
    end = jnp.broadcast_to(end_ref[...], (128, shots)).T[:, :1]
    distance = jnp.minimum(column - start, end - 1 - column)
    ramped = jnp.minimum((distance + 1).astype(jnp.float32) / EDGE, 1.0)
    weight = jnp.where(distance >= 0, ramped, 0.0) * -gain
    for freq in range(gathers_ref.shape[0]):
        for part in range(2):
            value = (gathers_ref[freq, part].astype(jnp.float32) * weight).astype(jnp.bfloat16)
            value = jnp.dot(value, origins, preferred_element_type=jnp.float32).astype(jnp.bfloat16)
            tapered_ref[freq, part] = value


def taper(gathers, aperture_start, aperture_end, taper_bin, taper_gain, origin):
    shots, points = gathers.shape[2:]
    return pl.pallas_call(
        taper_kernel,
        in_specs=[SCALARS, WHOLE, WHOLE, WHOLE, WHOLE, WHOLE],
        out_specs=WHOLE,
        out_shape=jax.ShapeDtypeStruct(gathers.shape, jnp.bfloat16),
        name="taper",
    )(
        taper_gain,
        aperture_start.reshape(1, shots),
        aperture_end.reshape(1, shots),
        taper_bin.reshape(1, points),
        origin.reshape(1, points),
        gathers,
    )


def pick_kernel(owner_ref, shares_ref, picked_ref):
    bins, blocks, _, own = picked_ref.shape
    for block in range(blocks):
        for unit in range(bins):
            span = slice(unit * own, (unit + 1) * own)
            picked_ref[unit, block] = shares_ref[owner_ref[block], :, span]


def pick(shares, block_owner, bins):
    _, width, receivers = shares.shape
    return pl.pallas_call(
        pick_kernel,
        in_specs=[SCALARS, WHOLE],
        out_specs=WHOLE,
        out_shape=jax.ShapeDtypeStruct((bins, BLOCKS, width, receivers // bins), jnp.bfloat16),
        cost_estimate=cost(PICK_FLOPS),
        name="pick",
    )(block_owner, shares)


def transpose_kernel(picked_ref, out_ref):
    bins, blocks, rows, own = picked_ref.shape
    width = blocks * rows
    for unit in range(bins):
        values = picked_ref[lax.bitwise_xor(lax.axis_index("rbin"), unit)].reshape(width, own)
        out_ref[:, unit * width : (unit + 1) * width] = values.T


def unit_product(r0, r1, g):
    def dot(a, b):
        return lax.dot_general(a, b, ROWS_BY_ROWS, preferred_element_type=jnp.float32)

    return dot(r0, g[0]) + dot(-r1, g[1]), dot(r0, g[1]) + dot(r1, g[0])


def choose(rbin, bins, freq, refs):
    values = [ref[freq] if len(ref.shape) == 4 else ref[...] for ref in refs]
    if len(values) == 1:
        return values[0]
    inner = jnp.logical_and(rbin > 0, rbin < bins - 1)
    return jnp.where(inner, values[0], values[1])


def early_kernel(order, n_operands, n_pieces, *refs):
    refs = list(refs)
    piece_refs = [refs.pop(0) for _ in range(n_pieces)]
    operands = [refs.pop(0) for _ in range(n_operands)]
    units = [[[operands[i] for i in unit] for unit in of_freq] for of_freq in order]
    out_ref, real_ref, imag_ref, left_ref, held, done, in_sems, out_sems = refs
    shot, rbin = lax.axis_index("shot"), lax.axis_index("rbin")
    copies = [
        pltpu.make_async_copy(ref, held.at[lax.bitwise_xor(shot, d)], in_sems.at[d])
        for d, ref in enumerate(piece_refs)
    ]
    for copy in copies:
        copy.start()
    for copy in copies:
        copy.wait()
    freqs = out_ref.shape[0]
    bins = max(len(of_freq) for of_freq in order)
    parts = n_pieces // (2 * freqs)
    own, width = held.shape[1], held.shape[2] // bins

    def recorded(freq, part, here, unit):
        span = slice(unit * width, (unit + 1) * width)
        first = (freq * 2 + part) * parts
        return jnp.concatenate([held[first + h, here, span] for h in range(parts)], axis=1)

    rows = min(own, ROWS)
    leaving = []
    for freq, of_freq in enumerate(units):
        for chunk in range(own // rows):
            here = slice(chunk * rows, (chunk + 1) * rows)
            real = imag = None
            for unit, candidates in enumerate(of_freq):
                g = choose(rbin, bins, freq, candidates)
                r0, r1 = recorded(freq, 0, here, unit), recorded(freq, 1, here, unit)
                a, b = unit_product(r0, r1, g)
                real = a if real is None else real + a
                imag = b if imag is None else imag + b
            if freq < freqs - 1:
                done[freq, here, 0, :] = real
                done[freq, here, 1, :] = imag
                leaving.append(
                    pltpu.make_async_copy(
                        done.at[freq, here], out_ref.at[freq, here], out_sems.at[freq, chunk]
                    )
                )
                leaving[-1].start()
            else:
                real_ref[here] = real
                imag_ref[here] = imag
                for part in range(2):
                    left_ref[part, here] = recorded(freq, part, here, bins - 1)
    for copy in leaving:
        copy.wait()


def late_kernel(bins, n_candidates, *refs):
    candidates = refs[:n_candidates]
    real_ref, imag_ref, left_ref, _, out_ref, done, sems = refs[n_candidates:]
    freq = out_ref.shape[0] - 1
    g = choose(lax.axis_index("rbin"), bins, freq, candidates)
    chunks = sems.shape[0]
    rows = real_ref.shape[0] // chunks
    leaving = []
    for chunk in range(chunks):
        here = slice(chunk * rows, (chunk + 1) * rows)
        a, b = unit_product(left_ref[0, here], left_ref[1, here], g)
        done[here, 0, :] = real_ref[here] + a
        done[here, 1, :] = imag_ref[here] + b
        leaving.append(
            pltpu.make_async_copy(done.at[here], out_ref.at[freq, here], sems.at[chunk])
        )
        leaving[-1].start()
    for copy in leaving:
        copy.wait()


def product(pieces, gathers):
    freqs, bins = len(gathers), len(gathers[0])
    shots, points = gathers[0][0][0].shape[-2:]
    n_pieces, (own, held_points) = len(pieces), pieces[0].shape
    chunks = own // min(own, ROWS)
    *full, last = gathers
    operands, order = [], []
    for of_freq in [*full, last[:-1]]:
        order.append([])
        for unit in of_freq:
            for value in unit:
                if not any(value is known for known in operands):
                    operands.append(value)
            order[-1].append([[value is o for o in operands].index(True) for value in unit])
    out_type = jax.ShapeDtypeStruct((freqs, own, 2, shots), jnp.float32)
    sum_type = jax.ShapeDtypeStruct((own, shots), jnp.float32)
    out, real, imag, left = pl.pallas_call(
        functools.partial(early_kernel, order, len(operands), n_pieces),
        in_specs=[IN_PLACE] * n_pieces + [WHOLE] * len(operands),
        out_specs=[IN_PLACE, WHOLE, WHOLE, WHOLE],
        out_shape=[
            out_type,
            sum_type,
            sum_type,
            jax.ShapeDtypeStruct((2, own, points), jnp.bfloat16),
        ],
        scratch_shapes=[
            pltpu.VMEM((n_pieces, own, held_points), jnp.bfloat16),
            pltpu.VMEM((freqs - 1, own, 2, shots), jnp.float32),
            pltpu.SemaphoreType.DMA((n_pieces,)),
            pltpu.SemaphoreType.DMA((freqs - 1, chunks)),
        ],
        compiler_params=pltpu.CompilerParams(vmem_limit_bytes=EARLY_BYTES),
        cost_estimate=cost(EARLY_FLOPS),
        name="early",
    )(*pieces, *operands)
    n_last = len(last[-1])
    return pl.pallas_call(
        functools.partial(late_kernel, bins, n_last),
        in_specs=[WHOLE] * (n_last + 3) + [IN_PLACE],
        out_specs=IN_PLACE,
        out_shape=out_type,
        scratch_shapes=[
            pltpu.VMEM((own, 2, shots), jnp.float32),
            pltpu.SemaphoreType.DMA((chunks,)),
        ],
        input_output_aliases={n_last + 3: 0},
        compiler_params=pltpu.CompilerParams(vmem_limit_bytes=LATE_BYTES),
        name="late",
    )(*last[-1], real, imag, left, out)


def per_device(
    local_gathers, recorded_shots, block_owner, aperture_start, aperture_end, taper_bin, taper_gain
):
    freqs, _, shots, points = local_gathers.shape
    rows, receivers = recorded_shots.shape[3:]
    slots = lax.axis_size("shot")
    bins = lax.axis_size("rbin")
    rbin = lax.axis_index("rbin")
    own = receivers // bins
    parts = slots // (2 * freqs)
    width = rows // parts

    shares = lax.all_to_all(recorded_shots[0].reshape(slots, width, receivers), "shot", 0, 0)
    picked = pick(shares, block_owner, bins)

    origin = np.arange(points, dtype=np.int32).reshape(BLOCKS, parts, width).transpose(1, 0, 2)
    tapered = taper(
        local_gathers, aperture_start, aperture_end, taper_bin, taper_gain, origin
    )
    if bins == 4:
        inner, outward = [(1, 2), (2, 1)], [(1, 0), (2, 3)]
        near = exchange(tapered, "rbin", 1)
        across = exchange(tapered, "rbin", 3, inner)
        picked = lax.all_to_all(picked, "rbin", 0, 0)
        second = exchange(across, "rbin", 1, outward)
        gathers = []
        ready, sent = picked, second
        for freq in range(freqs):
            crossed = exchange(after(near[freq], ready), "rbin", 3, inner)
            passed = exchange(after(crossed, sent), "rbin", 1, outward)
            gathers.append([[tapered], [near], [crossed, second], [across, passed]])
            ready, sent = crossed, passed
    else:
        picked = lax.all_to_all(picked, "rbin", 0, 0)
        gathers = [[[tapered]] + [[exchange(tapered, "rbin", d)] for d in range(1, bins)]] * freqs

    piece = pl.pallas_call(
        transpose_kernel,
        in_specs=[WHOLE],
        out_specs=WHOLE,
        out_shape=jax.ShapeDtypeStruct((own, bins * BLOCKS * width), jnp.bfloat16),
        name="turn",
    )(picked)
    pieces = []
    for d in range(0, slots, 2):
        other = piece if d == 0 else exchange(piece, "shot", d)
        pieces += [other, exchange(other, "shot", 1)]
    return product(pieces, gathers)


def solution(mesh):
    in_specs = (
        P(None, None, "shot", "rbin"),
        P("shot", None, None, "rbin", None),
        P(),
        P("shot"),
        P("shot"),
        P("rbin"),
        P(),
    )
    out_specs = P(None, "rbin", None, "shot")
    return jax.shard_map(
        per_device, mesh=mesh, in_specs=in_specs, out_specs=out_specs, check_vma=False
    )
```

```python
import functools

import jax
import jax.numpy as jnp
from jax import lax
from jax.experimental import pallas as pl
from jax.experimental.pallas import tpu as pltpu
from jax.sharding import PartitionSpec as P

BLOCKS = 4
EDGE = 64
LANES = 128
LABEL_ROWS = 16
PICK_FLOPS = 0 * 10**9
TAPER_FLOPS = 10**9
SUM_FLOPS = 4 * 10**9
LAST_FLOPS = 10**9
ROWS_BY_ROWS = (((1,), (1,)), ((), ()))
WHOLE = pl.BlockSpec(memory_space=pltpu.VMEM)
SCALARS = pl.BlockSpec(memory_space=pltpu.SMEM)
IN_PLACE = pl.BlockSpec(memory_space=pl.ANY)


def exchange(value, axis, distance, among=None):
    pairs = [(i ^ distance, i) for i in range(lax.axis_size(axis))]
    return lax.ppermute(value, axis, [p for p in pairs if among is None or p in among])


def after(value, *earlier):
    return lax.optimization_barrier((value, earlier))[0]


def settings(flops, megabytes=40):
    return {
        "cost_estimate": pl.CostEstimate(flops=flops, bytes_accessed=2**21, transcendentals=0),
        "compiler_params": pltpu.CompilerParams(vmem_limit_bytes=megabytes * 2**20),
    }


def unit_bin(unit):
    return lax.bitwise_xor(lax.axis_index("rbin"), unit)


def minus_weight(unit, gain_ref, start_ref, end_ref, bins_ref):
    shots, points = start_ref.shape[1], bins_ref.shape[1]
    labels = bins_ref[pl.ds(unit_bin(unit), 1), :].astype(jnp.int32)
    column = unit_bin(unit) * points + lax.broadcasted_iota(jnp.int32, labels.shape, 1)
    gain = jnp.zeros(labels.shape, jnp.float32)
    for label in range(gain_ref.shape[0]):
        gain = gain + jnp.where(labels == label, gain_ref[label], 0.0)
    start = jnp.broadcast_to(start_ref[...], (LANES, shots)).T[:, :1]
    end = jnp.broadcast_to(end_ref[...], (LANES, shots)).T[:, :1]
    distance = jnp.minimum(column - start, end - 1 - column)
    ramped = jnp.minimum((distance + 1).astype(jnp.float32) / EDGE, 1.0)
    return jnp.where(distance >= 0, ramped, 0.0) * -gain


def tapered(values, weight):
    return (values.astype(jnp.float32) * weight).astype(jnp.bfloat16)


def taper_kernel(units, gain_ref, start_ref, end_ref, bins_ref, *refs):
    for unit, raw_ref, out_ref in zip(units, refs[: len(units)], refs[len(units) :]):
        weight = minus_weight(unit, gain_ref, start_ref, end_ref, bins_ref)
        for freq in range(raw_ref.shape[0]):
            for part in range(2):
                out_ref[freq, part] = tapered(raw_ref[freq, part], weight)


def taper(units, raw, taper_args):
    return pl.pallas_call(
        functools.partial(taper_kernel, units),
        in_specs=[SCALARS] + [WHOLE] * (3 + len(raw)),
        out_specs=[WHOLE] * len(raw),
        out_shape=[jax.ShapeDtypeStruct(r.shape, r.dtype) for r in raw],
        name="taper",
        **settings(TAPER_FLOPS, 16),
    )(*taper_args, *raw)


def share_kernel(bins, recorded_ref, shares_ref):
    _, freqs, _, _, receivers = recorded_ref.shape
    parts = shares_ref.shape[0] // (2 * freqs)
    own = receivers // bins
    part = own // parts
    for slot in range(shares_ref.shape[0]):
        for unit in range(bins):
            first = unit * own + slot % parts * part
            shares_ref[slot, :, unit * part : (unit + 1) * part] = recorded_ref[
                0, slot // parts // 2, slot // parts % 2, :, first : first + part
            ]


def pick_kernel(owner_ref, bin_ref, shares_ref, picked_ref):
    bins, points, part = picked_ref.shape
    points -= LABEL_ROWS
    rows = points // BLOCKS
    labels = jnp.broadcast_to(bin_ref[...].astype(jnp.float32), (LABEL_ROWS, part))
    for unit in range(bins):
        span = slice(unit * part, (unit + 1) * part)
        for block in range(BLOCKS):
            here = slice(block * rows, (block + 1) * rows)
            picked_ref[unit, here] = shares_ref[owner_ref[block], :, span]
        picked_ref[unit, points:] = labels.astype(jnp.bfloat16)


def wanted_shares(recorded, block_owner, taper_bin, bins):
    _, freqs, _, rows, receivers = recorded.shape
    slots = lax.axis_size("shot")
    parts = slots // (2 * freqs)
    part = receivers // bins // parts
    points = BLOCKS * rows
    if part != points:
        shares = recorded.reshape(freqs, 2, rows, bins, parts, part)
        shares = shares.transpose(0, 1, 4, 3, 2, 5).reshape(slots, bins, rows, part)
        shares = lax.all_to_all(shares, "shot", 0, 0)
        picked = shares[block_owner].transpose(1, 0, 2, 3).reshape(bins, points, part)
        picked = lax.all_to_all(picked, "rbin", 0, 0)
        labels = lax.all_gather(taper_bin, "rbin").astype(jnp.float32)
        return turn(picked, points)[0], labels
    shares = pl.pallas_call(
        functools.partial(share_kernel, bins),
        in_specs=[WHOLE],
        out_specs=WHOLE,
        out_shape=jax.ShapeDtypeStruct((slots, rows, bins * part), recorded.dtype),
        name="share",
        **settings(0, 8),
    )(recorded)
    shares = lax.all_to_all(shares, "shot", 0, 0)
    picked = pl.pallas_call(
        pick_kernel,
        in_specs=[SCALARS, WHOLE, WHOLE],
        out_specs=WHOLE,
        out_shape=jax.ShapeDtypeStruct((bins, points + LABEL_ROWS, part), recorded.dtype),
        name="pick",
        **settings(PICK_FLOPS, 8),
    )(block_owner, taper_bin.reshape(1, points), shares)
    return turn(lax.all_to_all(picked, "rbin", 0, 0), points)


def turn_kernel(picked_ref, out_ref, labels_ref):
    bins, points = labels_ref.shape
    for unit in range(bins):
        values = picked_ref[unit_bin(unit), :points]
        out_ref[:, unit * points : (unit + 1) * points] = values.T
        if picked_ref.shape[1] > points:
            labels_ref[unit : unit + 1] = picked_ref[unit, points:][:1].astype(jnp.float32)


def turn(picked, points):
    bins, _, part = picked.shape
    return pl.pallas_call(
        turn_kernel,
        in_specs=[WHOLE],
        out_specs=[WHOLE, WHOLE],
        out_shape=[
            jax.ShapeDtypeStruct((part, bins * points), jnp.bfloat16),
            jax.ShapeDtypeStruct((bins, points), jnp.float32),
        ],
        name="turn",
        **settings(0, 8),
    )(picked)


def unit_product(r0, r1, g):
    def dot(a, b):
        return lax.dot_general(a, b, ROWS_BY_ROWS, preferred_element_type=jnp.float32)

    return dot(r0, g[0]) + dot(-r1, g[1]), dot(r0, g[1]) + dot(r1, g[0])


def choose(bins, freq, refs):
    values = [ref[freq] if len(ref.shape) == 4 else ref[...] for ref in refs]
    if len(values) == 1:
        return values[0]
    rbin = lax.axis_index("rbin")
    inner = jnp.logical_and(rbin > 0, rbin < bins - 1)
    return jnp.where(inner, values[0], values[1])


def sum_kernel(freqs, order, raw_units, n_operands, splits, *refs):
    refs = list(refs)
    piece_refs = [[refs.pop(0) for _ in range(n)] for n in splits]
    taper_refs = [refs.pop(0) for _ in range(4)]
    operands = [refs.pop(0) for _ in range(n_operands)]
    sums = [[refs.pop(0) for _ in range(3)] for _ in range(freqs)]
    weight_ref, held, ready, sems = refs
    shot = lax.axis_index("shot")
    copies = []
    for d, blocks in enumerate(piece_refs):
        for i, ref in enumerate(blocks):
            here = pl.ds(i * ref.shape[0], ref.shape[0])
            target = held.at[lax.bitwise_xor(shot, d), here]
            copies.append(pltpu.make_async_copy(ref, target, sems.at[d, i]))
    for copy in copies:
        copy.start()
    bins = len(order[0]) + 1
    points = weight_ref.shape[1]
    parts = len(splits) // (2 * freqs)
    part = held.shape[1]
    weight_ref[...] = minus_weight(bins - 1, *taper_refs)
    for at, unit in enumerate(raw_units):
        weight = minus_weight(unit, *taper_refs)
        for freq in range(freqs):
            values = choose(bins, freq, [operands[i] for i in order[freq][unit]])
            for c in range(2):
                ready[at, freq, c] = tapered(values[c], weight)
    for copy in copies:
        copy.wait()
    for freq in range(freqs):
        real_ref, imag_ref, left_ref = sums[freq]
        for h in range(parts):
            here = slice(h * part, (h + 1) * part)
            first = freq * 2 * parts + h
            real = imag = None
            for unit, candidates in enumerate(order[freq]):
                if unit in raw_units:
                    g = ready[raw_units.index(unit), freq]
                else:
                    g = choose(bins, freq, [operands[i] for i in candidates])
                span = slice(unit * points, (unit + 1) * points)
                a, b = unit_product(held[first, :, span], held[first + parts, :, span], g)
                real = a if real is None else real + a
                imag = b if imag is None else imag + b
            real_ref[here] = real
            imag_ref[here] = imag
            span = slice((bins - 1) * points, bins * points)
            for c in range(2):
                left_ref[c, here] = held[first + c * parts, :, span]


def last_kernel(bins, freq, n_candidates, *refs):
    candidates = refs[:n_candidates]
    real_ref, imag_ref, left_ref, weight_ref = refs[n_candidates : n_candidates + 4]
    out_ref, done, sems = refs[-3:]
    values = choose(bins, freq, candidates)
    g = [tapered(values[c], weight_ref[...]) for c in range(2)]
    chunks = sems.shape[0]
    rows = real_ref.shape[0] // chunks
    leaving = []
    for chunk in range(chunks):
        here = slice(chunk * rows, (chunk + 1) * rows)
        a, b = unit_product(left_ref[0, here], left_ref[1, here], g)
        done[here, 0, :] = real_ref[here] + a
        done[here, 1, :] = imag_ref[here] + b
        leaving.append(
            pltpu.make_async_copy(done.at[here], out_ref.at[freq, here], sems.at[chunk])
        )
        leaving[-1].start()
    for copy in leaving:
        copy.wait()


def product(pieces, gathers, raw_units, taper_args):
    freqs, bins = len(gathers), len(gathers[0])
    shots, points = gathers[0][0][0].shape[-2:]
    splits = [len(blocks) for blocks in pieces]
    blocks = [block for blocks in pieces for block in blocks]
    part = pieces[0][0].shape[0]
    own = part * len(pieces) // (2 * freqs)
    operands, order = [], []
    for of_freq in gathers:
        order.append([])
        for unit in of_freq[:-1]:
            for value in unit:
                if not any(value is known for known in operands):
                    operands.append(value)
            order[-1].append([[value is o for o in operands].index(True) for value in unit])
    sum_type = jax.ShapeDtypeStruct((own, shots), jnp.float32)
    left_type = jax.ShapeDtypeStruct((2, own, points), jnp.bfloat16)
    *sums, weight = pl.pallas_call(
        functools.partial(sum_kernel, freqs, order, raw_units, len(operands), splits),
        in_specs=[IN_PLACE] * len(blocks) + [SCALARS] + [WHOLE] * (3 + len(operands)),
        out_specs=[WHOLE] * (3 * freqs + 1),
        out_shape=[sum_type, sum_type, left_type] * freqs
        + [jax.ShapeDtypeStruct((shots, points), jnp.float32)],
        scratch_shapes=[
            pltpu.VMEM((len(pieces), part, bins * points), jnp.bfloat16),
            pltpu.VMEM((max(1, len(raw_units)), freqs, 2, shots, points), jnp.bfloat16),
            pltpu.SemaphoreType.DMA((len(pieces), max(splits))),
        ],
        name="sum",
        **settings(SUM_FLOPS),
    )(*blocks, *taper_args, *operands)
    chunks = 2
    out = []
    for freq in range(freqs):
        candidates = gathers[freq][-1]
        n = len(candidates)
        out = pl.pallas_call(
            functools.partial(last_kernel, bins, freq, n),
            in_specs=[WHOLE] * (n + 4) + [IN_PLACE] * len(out),
            out_specs=[IN_PLACE],
            out_shape=[jax.ShapeDtypeStruct((freqs, own, 2, shots), jnp.float32)],
            scratch_shapes=[
                pltpu.VMEM((own, 2, shots), jnp.float32),
                pltpu.SemaphoreType.DMA((chunks,)),
            ],
            input_output_aliases={n + 4: 0} if out else {},
            name="last",
            **settings(LAST_FLOPS, 16),
        )(*candidates, *sums[3 * freq : 3 * freq + 3], weight, *out)
    return out[0]


def per_device(
    local_gathers, recorded_shots, block_owner, aperture_start, aperture_end, taper_bin, taper_gain
):
    freqs, _, shots, points = local_gathers.shape
    slots = lax.axis_size("shot")
    bins = lax.axis_size("rbin")

    piece, labels = wanted_shares(recorded_shots, block_owner, taper_bin, bins)
    taper_args = (
        taper_gain,
        aperture_start.reshape(1, shots),
        aperture_end.reshape(1, shots),
        labels,
    )

    if bins == 4:
        inner, outward = [(1, 2), (2, 1)], [(1, 0), (2, 3)]
        near = exchange(local_gathers, "rbin", 1)
        across = exchange(local_gathers, "rbin", 3, inner)
        second = exchange(across, "rbin", 1, outward)
        units = taper([0, 1], [local_gathers, near], taper_args)
        over, down, corner = [exchange(piece, "shot", d) for d in (2, 4, 6)]
        beside = exchange(piece, "shot", 1)
        first = exchange(after(near[0], across), "rbin", 3, inner)
        near_1 = after(near[1], first)
        first_g, second, units = lax.optimization_barrier((first, second, units))
        passed_0 = exchange(first_g, "rbin", 1, outward)
        other = exchange(near_1, "rbin", 3, inner)
        over, down, corner = lax.optimization_barrier((over, down, corner))
        passed_1 = exchange(other, "rbin", 1, outward)
        pieces = [[piece], [beside]]
        for value in (over, down, corner):
            pieces += [[value], [exchange(value, "shot", 1)]]
        gathers = [
            [[units[0]], [units[1]], [first, second], [across, passed_0]],
            [[units[0]], [units[1]], [other, second], [across, passed_1]],
        ]
        pieces[0] = [after(piece, passed_0)]
        return product(pieces, gathers, [2], taper_args)
    else:
        raw = [local_gathers] + [exchange(local_gathers, "rbin", d) for d in range(1, bins)]
        units = [taper([d], [raw[d]], taper_args)[0] for d in range(bins - 1)] + [raw[-1]]
        gathers = [[[unit] for unit in units]] * freqs
        raw_units = []

    if slots == 8:
        half = piece.shape[0] // 2
        over = exchange(piece, "shot", 2)
        down = exchange(piece, "shot", 4)
        corner = [exchange(over[:half], "shot", 4), exchange(down[half:], "shot", 2)]
        pieces = {0: [piece], 2: [over], 4: [down], 6: corner}
    else:
        pieces = {d: [exchange(piece, "shot", d) if d else piece] for d in range(0, slots, 2)}
    for d in range(0, slots, 2):
        pieces[d + 1] = [exchange(p, "shot", 1) for p in pieces[d]]
    pieces = [pieces[d] for d in range(slots)]
    return product(pieces, gathers, raw_units, taper_args)


def solution(mesh):
    in_specs = (
        P(None, None, "shot", "rbin"),
        P("shot", None, None, "rbin", None),
        P(),
        P("shot"),
        P("shot"),
        P("rbin"),
        P(),
    )
    out_specs = P(None, "rbin", None, "shot")
    return jax.shard_map(
        per_device, mesh=mesh, in_specs=in_specs, out_specs=out_specs, check_vma=False
    )
```

```python
import functools

import jax
import jax.numpy as jnp
from jax import lax
from jax.experimental import pallas as pl
from jax.experimental.pallas import tpu as pltpu
from jax.sharding import PartitionSpec as P

BLOCKS = 4
EDGE = 64
LANES = 128
LABEL_ROWS = 16
PICK_FLOPS = 0
TAPER_FLOPS = 10**9
SUM_FLOPS = 12 * 10**9
LAST_FLOPS = 10**9
ROWS_BY_ROWS = (((1,), (1,)), ((), ()))
WHOLE = pl.BlockSpec(memory_space=pltpu.VMEM)
SCALARS = pl.BlockSpec(memory_space=pltpu.SMEM)
IN_PLACE = pl.BlockSpec(memory_space=pl.ANY)


def exchange(value, axis, distance, among=None):
    pairs = [(i ^ distance, i) for i in range(lax.axis_size(axis))]
    return lax.ppermute(value, axis, [p for p in pairs if among is None or p in among])


def after(value, *earlier):
    return lax.optimization_barrier((value, earlier))[0]


def settings(flops, megabytes=40):
    return {
        "cost_estimate": pl.CostEstimate(flops=flops, bytes_accessed=2**21, transcendentals=0),
        "compiler_params": pltpu.CompilerParams(vmem_limit_bytes=megabytes * 2**20),
    }


def unit_bin(unit):
    return lax.bitwise_xor(lax.axis_index("rbin"), unit)


def minus_weight(unit, gain_ref, start_ref, end_ref, bins_ref):
    shots, points = start_ref.shape[1], bins_ref.shape[1]
    labels = bins_ref[pl.ds(unit_bin(unit), 1), :].astype(jnp.int32)
    column = unit_bin(unit) * points + lax.broadcasted_iota(jnp.int32, labels.shape, 1)
    gain = jnp.zeros(labels.shape, jnp.float32)
    for label in range(gain_ref.shape[0]):
        gain = gain + jnp.where(labels == label, gain_ref[label], 0.0)
    start = jnp.broadcast_to(start_ref[...], (LANES, shots)).T[:, :1]
    end = jnp.broadcast_to(end_ref[...], (LANES, shots)).T[:, :1]
    distance = jnp.minimum(column - start, end - 1 - column)
    ramped = jnp.minimum((distance + 1).astype(jnp.float32) / EDGE, 1.0)
    return jnp.where(distance >= 0, ramped, 0.0) * -gain


def tapered(values, weight):
    return (values.astype(jnp.float32) * weight).astype(jnp.bfloat16)


def taper_kernel(units, gain_ref, start_ref, end_ref, bins_ref, *refs):
    for unit, raw_ref, out_ref in zip(units, refs[: len(units)], refs[len(units) :]):
        weight = minus_weight(unit, gain_ref, start_ref, end_ref, bins_ref)
        for freq in range(raw_ref.shape[0]):
            for part in range(2):
                out_ref[freq, part] = tapered(raw_ref[freq, part], weight)


def taper(units, raw, taper_args):
    return pl.pallas_call(
        functools.partial(taper_kernel, units),
        in_specs=[SCALARS] + [WHOLE] * (3 + len(raw)),
        out_specs=[WHOLE] * len(raw),
        out_shape=[jax.ShapeDtypeStruct(r.shape, r.dtype) for r in raw],
        name="taper",
        **settings(TAPER_FLOPS, 16),
    )(*taper_args, *raw)


def share_kernel(bins, recorded_ref, shares_ref):
    _, freqs, _, _, receivers = recorded_ref.shape
    parts = shares_ref.shape[0] // (2 * freqs)
    own = receivers // bins
    part = own // parts
    for slot in range(shares_ref.shape[0]):
        for unit in range(bins):
            first = unit * own + slot % parts * part
            shares_ref[slot, :, unit * part : (unit + 1) * part] = recorded_ref[
                0, slot // parts // 2, slot // parts % 2, :, first : first + part
            ]


def pick_kernel(owner_ref, bin_ref, shares_ref, picked_ref):
    bins, points, part = picked_ref.shape
    points -= LABEL_ROWS
    rows = points // BLOCKS
    labels = jnp.broadcast_to(bin_ref[...].astype(jnp.float32), (LABEL_ROWS, part))
    for unit in range(bins):
        span = slice(unit * part, (unit + 1) * part)
        for block in range(BLOCKS):
            here = slice(block * rows, (block + 1) * rows)
            picked_ref[unit, here] = shares_ref[owner_ref[block], :, span]
        picked_ref[unit, points:] = labels.astype(jnp.bfloat16)


def wanted_shares(recorded, block_owner, taper_bin, bins):
    _, freqs, _, rows, receivers = recorded.shape
    slots = lax.axis_size("shot")
    parts = slots // (2 * freqs)
    part = receivers // bins // parts
    points = BLOCKS * rows
    if part != points:
        shares = recorded.reshape(freqs, 2, rows, bins, parts, part)
        shares = shares.transpose(0, 1, 4, 3, 2, 5).reshape(slots, bins, rows, part)
        shares = lax.all_to_all(shares, "shot", 0, 0)
        picked = shares[block_owner].transpose(1, 0, 2, 3).reshape(bins, points, part)
        picked = lax.all_to_all(picked, "rbin", 0, 0)
        labels = lax.all_gather(taper_bin, "rbin").astype(jnp.float32)
        return turn(picked, points)[0], labels
    shares = pl.pallas_call(
        functools.partial(share_kernel, bins),
        in_specs=[WHOLE],
        out_specs=WHOLE,
        out_shape=jax.ShapeDtypeStruct((slots, rows, bins * part), recorded.dtype),
        name="share",
        **settings(0, 8),
    )(recorded)
    shares = lax.all_to_all(shares, "shot", 0, 0)
    picked = pl.pallas_call(
        pick_kernel,
        in_specs=[SCALARS, WHOLE, WHOLE],
        out_specs=WHOLE,
        out_shape=jax.ShapeDtypeStruct((bins, points + LABEL_ROWS, part), recorded.dtype),
        name="pick",
        **settings(PICK_FLOPS, 8),
    )(block_owner, taper_bin.reshape(1, points), shares)
    return turn(lax.all_to_all(picked, "rbin", 0, 0), points)


def turn_kernel(picked_ref, out_ref, labels_ref):
    bins, points = labels_ref.shape
    for unit in range(bins):
        values = picked_ref[unit_bin(unit), :points]
        out_ref[:, unit * points : (unit + 1) * points] = values.T
        if picked_ref.shape[1] > points:
            labels_ref[unit : unit + 1] = picked_ref[unit, points:][:1].astype(jnp.float32)


def turn(picked, points):
    bins, _, part = picked.shape
    return pl.pallas_call(
        turn_kernel,
        in_specs=[WHOLE],
        out_specs=[WHOLE, WHOLE],
        out_shape=[
            jax.ShapeDtypeStruct((part, bins * points), jnp.bfloat16),
            jax.ShapeDtypeStruct((bins, points), jnp.float32),
        ],
        name="turn",
        **settings(0, 8),
    )(picked)


def unit_product(r0, r1, g):
    def dot(a, b):
        return lax.dot_general(a, b, ROWS_BY_ROWS, preferred_element_type=jnp.float32)

    return dot(r0, g[0]) + dot(-r1, g[1]), dot(r0, g[1]) + dot(r1, g[0])


def choose(bins, freq, refs):
    values = [ref[freq] if len(ref.shape) == 4 else ref[...] for ref in refs]
    if len(values) == 1:
        return values[0]
    rbin = lax.axis_index("rbin")
    inner = jnp.logical_and(rbin > 0, rbin < bins - 1)
    return jnp.where(inner, values[0], values[1])


def sum_kernel(freqs, order, raw_units, n_operands, splits, *refs):
    refs = list(refs)
    piece_refs = [[refs.pop(0) for _ in range(n)] for n in splits]
    taper_refs = [refs.pop(0) for _ in range(4)]
    operands = [refs.pop(0) for _ in range(n_operands)]
    sums = [[refs.pop(0) for _ in range(3)] for _ in range(freqs)]
    weight_ref, held, ready, sems = refs
    shot = lax.axis_index("shot")
    copies = []
    for d, blocks in enumerate(piece_refs):
        for i, ref in enumerate(blocks):
            here = pl.ds(i * ref.shape[0], ref.shape[0])
            target = held.at[lax.bitwise_xor(shot, d), here]
            copies.append(pltpu.make_async_copy(ref, target, sems.at[d, i]))
    for copy in copies:
        copy.start()
    bins = len(order[0]) + 1
    points = weight_ref.shape[1]
    parts = len(splits) // (2 * freqs)
    part = held.shape[1]
    weight_ref[...] = minus_weight(bins - 1, *taper_refs)
    for at, unit in enumerate(raw_units):
        weight = minus_weight(unit, *taper_refs)
        for freq in range(freqs):
            values = choose(bins, freq, [operands[i] for i in order[freq][unit]])
            for c in range(2):
                ready[at, freq, c] = tapered(values[c], weight)
    for copy in copies:
        copy.wait()
    for freq in range(freqs):
        real_ref, imag_ref, left_ref = sums[freq]
        for h in range(parts):
            here = slice(h * part, (h + 1) * part)
            first = freq * 2 * parts + h
            real = imag = None
            for unit, candidates in enumerate(order[freq]):
                if unit in raw_units:
                    g = ready[raw_units.index(unit), freq]
                else:
                    g = choose(bins, freq, [operands[i] for i in candidates])
                span = slice(unit * points, (unit + 1) * points)
                a, b = unit_product(held[first, :, span], held[first + parts, :, span], g)
                real = a if real is None else real + a
                imag = b if imag is None else imag + b
            real_ref[here] = real
            imag_ref[here] = imag
            span = slice((bins - 1) * points, bins * points)
            for c in range(2):
                left_ref[c, here] = held[first + c * parts, :, span]


def last_kernel(bins, freq, n_candidates, *refs):
    candidates = refs[:n_candidates]
    real_ref, imag_ref, left_ref, weight_ref = refs[n_candidates : n_candidates + 4]
    out_ref, done, sems = refs[-3:]
    values = choose(bins, freq, candidates)
    g = [tapered(values[c], weight_ref[...]) for c in range(2)]
    chunks = sems.shape[0]
    rows = real_ref.shape[0] // chunks
    leaving = []
    for chunk in range(chunks):
        here = slice(chunk * rows, (chunk + 1) * rows)
        a, b = unit_product(left_ref[0, here], left_ref[1, here], g)
        done[here, 0, :] = real_ref[here] + a
        done[here, 1, :] = imag_ref[here] + b
        leaving.append(
            pltpu.make_async_copy(done.at[here], out_ref.at[freq, here], sems.at[chunk])
        )
        leaving[-1].start()
    for copy in leaving:
        copy.wait()


def product(pieces, gathers, raw_units, taper_args):
    freqs, bins = len(gathers), len(gathers[0])
    shots, points = gathers[0][0][0].shape[-2:]
    splits = [len(blocks) for blocks in pieces]
    blocks = [block for blocks in pieces for block in blocks]
    part = pieces[0][0].shape[0]
    own = part * len(pieces) // (2 * freqs)
    operands, order = [], []
    for of_freq in gathers:
        order.append([])
        for unit in of_freq[:-1]:
            for value in unit:
                if not any(value is known for known in operands):
                    operands.append(value)
            order[-1].append([[value is o for o in operands].index(True) for value in unit])
    sum_type = jax.ShapeDtypeStruct((own, shots), jnp.float32)
    left_type = jax.ShapeDtypeStruct((2, own, points), jnp.bfloat16)
    *sums, weight = pl.pallas_call(
        functools.partial(sum_kernel, freqs, order, raw_units, len(operands), splits),
        in_specs=[IN_PLACE] * len(blocks) + [SCALARS] + [WHOLE] * (3 + len(operands)),
        out_specs=[WHOLE] * (3 * freqs + 1),
        out_shape=[sum_type, sum_type, left_type] * freqs
        + [jax.ShapeDtypeStruct((shots, points), jnp.float32)],
        scratch_shapes=[
            pltpu.VMEM((len(pieces), part, bins * points), jnp.bfloat16),
            pltpu.VMEM((max(1, len(raw_units)), freqs, 2, shots, points), jnp.bfloat16),
            pltpu.SemaphoreType.DMA((len(pieces), max(splits))),
        ],
        name="sum",
        **settings(SUM_FLOPS),
    )(*blocks, *taper_args, *operands)
    chunks = 2
    out = []
    for freq in range(freqs):
        candidates = gathers[freq][-1]
        n = len(candidates)
        out = pl.pallas_call(
            functools.partial(last_kernel, bins, freq, n),
            in_specs=[WHOLE] * (n + 4) + [IN_PLACE] * len(out),
            out_specs=[IN_PLACE],
            out_shape=[jax.ShapeDtypeStruct((freqs, own, 2, shots), jnp.float32)],
            scratch_shapes=[
                pltpu.VMEM((own, 2, shots), jnp.float32),
                pltpu.SemaphoreType.DMA((chunks,)),
            ],
            input_output_aliases={n + 4: 0} if out else {},
            name="last",
            **settings(LAST_FLOPS, 16),
        )(*candidates, *sums[3 * freq : 3 * freq + 3], weight, *out)
    return out[0]


def per_device(
    local_gathers, recorded_shots, block_owner, aperture_start, aperture_end, taper_bin, taper_gain
):
    freqs, _, shots, points = local_gathers.shape
    slots = lax.axis_size("shot")
    bins = lax.axis_size("rbin")

    piece, labels = wanted_shares(recorded_shots, block_owner, taper_bin, bins)
    taper_args = (
        taper_gain,
        aperture_start.reshape(1, shots),
        aperture_end.reshape(1, shots),
        labels,
    )

    if (bins, slots, freqs) == (4, 8, 2):
        return short_way(local_gathers, piece, taper_args)
    raw = [local_gathers] + [exchange(local_gathers, "rbin", d) for d in range(1, bins)]
    units = [taper([d], [raw[d]], taper_args)[0] for d in range(bins - 1)] + [raw[-1]]
    pieces = []
    for d in range(0, slots, 2):
        value = exchange(piece, "shot", d) if d else piece
        pieces += [[value], [exchange(value, "shot", 1)]]
    return product(pieces, [[[unit] for unit in units]] * freqs, [], taper_args)


def short_way(local_gathers, piece, taper_args):
    inner, outward = [(1, 2), (2, 1)], [(1, 0), (2, 3)]
    near = exchange(local_gathers, "rbin", 1)
    across = exchange(local_gathers, "rbin", 3, inner)
    second = exchange(across, "rbin", 1, outward)
    units = taper([0, 1], [local_gathers, near], taper_args)
    over, down, corner = [exchange(piece, "shot", d) for d in (2, 4, 6)]
    beside = exchange(piece, "shot", 1)
    crossed_0 = exchange(after(near[0], across), "rbin", 3, inner)
    near_1 = after(near[1], crossed_0)
    to_pass, second, units, beside = lax.optimization_barrier((crossed_0, second, units, beside))
    passed_0 = exchange(to_pass, "rbin", 1, outward)
    crossed_1 = exchange(near_1, "rbin", 3, inner)
    over, down, corner = lax.optimization_barrier((over, down, corner))
    passed_1 = exchange(crossed_1, "rbin", 1, outward)
    pieces = [[after(piece, passed_0)], [beside]]
    for value in (over, down, corner):
        pieces += [[value], [exchange(value, "shot", 1)]]
    gathers = [
        [[units[0]], [units[1]], [crossed_0, second], [across, passed_0]],
        [[units[0]], [units[1]], [crossed_1, second], [across, passed_1]],
    ]
    return product(pieces, gathers, [2], taper_args)


def solution(mesh):
    in_specs = (
        P(None, None, "shot", "rbin"),
        P("shot", None, None, "rbin", None),
        P(),
        P("shot"),
        P("shot"),
        P("rbin"),
        P(),
    )
    out_specs = P(None, "rbin", None, "shot")
    return jax.shard_map(
        per_device, mesh=mesh, in_specs=in_specs, out_specs=out_specs, check_vma=False
    )
```
